32 devices in a mesh: parts: 2 (over y), dp: 4 (over z), tp: 4 (over x, core).
Axes of the slice: x: 2, y: 2, z: 4, core: 2. Of those that a mesh axis runs over, the one named last changes fastest.
Arguments:
- memory_hidden: bfloat16 [512, 5120], P(('parts', 'dp'), 'tp'), parts along dimension 0, may hold values from -6 to 6
- kv_weight: bfloat16 [2, 5120, 1024], P(None, None, 'tp'), may hold values from -0.078125 to 0.078125
- kv_bias: bfloat16 [2, 1024], P(None, 'tp'), may hold values from -3 to 3
- memory_sections: int32 [512], P('parts'), parts along dimension 0, may hold values from 0 to 3, never falling along the last dimension, each value on 1 to 128 neighbouring positions
- group_sections: int32 [8], P(('parts', 'dp')), parts along dimension 0, may hold values from 0 to 3
- queries: bfloat16 [64, 5120], P(('parts', 'dp'), 'tp'), parts along dimension 0, may hold values from -130 to 130
- new_keys: bfloat16 [64, 1024], P(('parts', 'dp'), 'tp'), parts along dimension 0, may hold values from -5 to 5
- new_values: bfloat16 [64, 1024], P(('parts', 'dp'), 'tp'), parts along dimension 0, may hold values from -5 to 5
- cache_keys: bfloat16 [32, 512, 1024], P(('parts', 'dp'), None, 'tp'), parts along dimension 0, may hold values from -5 to 5
- cache_values: bfloat16 [32, 512, 1024], P(('parts', 'dp'), None, 'tp'), parts along dimension 0, may hold values from -5 to 5
- cache_lengths: int32 [32], P(('parts', 'dp')), parts along dimension 0, may hold values from 2 to 512, as said below
- out_weight: bfloat16 [5120, 5120], P('tp', 'dp'), may hold values from -1.25 to 1.25
Outputs:
- output: bfloat16 [64, 5120], P(('parts', 'tp'), 'dp'), parts along dimension 0
The draws below stay inside these ranges and needn't reach their ends.
There are 2 independent parts, one for each index of `parts`. The reference program is written for one: setup_inputs(seed, part) draws one part's arguments, and reference() takes and returns one part's arrays. A program takes and returns all parts, laid end to end along the dimension named above; an argument that names none is the same for every part. Nothing has to cross between parts.
Inputs may be any that keep to these rules, and one draw needn't show every extreme that they name: `memory_sections`: memory rows are grouped by section in order; every section holds at least one row. `cache_lengths`: some request has all 512 slots live.
All inputs are finite; a program needn't handle non-finite values.
Results may differ from the reference program's by a relative error of at most 0.0054.
Values may be sent and summed in bfloat16 or wider, within the bound.
A program may use at most 64 MiB of HBM per device.

```python
import math
import jax
import jax.numpy as jnp
import numpy as np
from jax import lax

D = 5120
HQ = 40
KVH = 8
HD = 128
MROWS = 256
SECTIONS = 4
NEW = 2
REQ_DEV = 4
LMAX = 512
GROUPS = 4
REQUESTS = 16
ROWS = 32


def common_keys(key):
    return jax.random.truncated_normal(jax.random.fold_in(key, 101), -5.0, 5.0, (REQUESTS, LMAX, KVH * HD), jnp.float32)


def draw_cache_keys(key, part):
    keys = common_keys(key)
    return keys.astype(jnp.bfloat16)


def draw_queries(key, part):
    drawn = jax.random.truncated_normal(jax.random.fold_in(key, 103), -6.0, 6.0, (ROWS, HQ * HD), jnp.float32)
    return drawn.astype(jnp.bfloat16)


def draw_cache_lengths(key, part):
    shift = jax.random.randint(jax.random.fold_in(key, 105), (GROUPS,), 0, 4)
    caps = jnp.maximum(LMAX // jnp.power(2, shift), 2)
    per_request = jnp.repeat(caps, REQ_DEV, total_repeat_length=REQUESTS)
    lengths = jax.random.randint(jax.random.fold_in(key, 106), (REQUESTS,), 2, per_request + 1)
    longest = jax.random.randint(jax.random.fold_in(key, 107), (), 0, REQUESTS)
    return jnp.where(jnp.arange(REQUESTS) == longest, LMAX, lengths).astype(jnp.int32)


def plant(drawn, key, least, largest):
    longest = drawn.shape.index(max(drawn.shape))
    spots = []
    for shift in (0, 1):
        where = [jax.random.randint(jax.random.fold_in(key, axis), (), 0, length) for axis, length in enumerate(drawn.shape)]
        where[longest] = (where[longest] + shift) % drawn.shape[longest]
        spots.append(tuple(where))
    return drawn.at[spots[0]].set(least).at[spots[1]].set(largest)


def block_scale(key, extent, cuts, smallest, largest):
    gain = 1.0
    for dim, blocks in cuts:
        steps = jax.random.uniform(jax.random.fold_in(jax.random.fold_in(key, 6), dim), (blocks,), jnp.float32, smallest / len(cuts), largest / len(cuts))
        gain = gain * jnp.repeat(jnp.exp(steps), extent[dim] // blocks).reshape((-1,) + (1,) * (len(extent) - 1 - dim))
    return gain


def split_up(number_of, total, bound, skew):
    loads = [(1 << 20) // math.isqrt(rank ** skew) + 1 for rank in range(2, number_of + 1)]
    rest, counts = total - bound - (number_of - 1), [1] * (number_of - 1)
    while rest > 0:
        movable = [i for i in range(number_of - 1) if counts[i] < bound]
        whole, left = sum([loads[i] for i in movable]), rest
        for i in movable:
            more = min(bound - counts[i], max(1, left * loads[i] // whole), rest)
            counts[i] = counts[i] + more
            rest = rest - more
    return np.array([bound] + counts)


def ragged_sizes(rng, number_of, total, reach, skew):
    if number_of == 2:
        one = jax.random.randint(rng, (), max(1, total - reach), min(reach, total - 1) + 1)
        return jnp.stack([one, total - one])
    tallies = jnp.asarray(split_up(number_of, total, reach, skew), jnp.int32)
    couples = (number_of - 1) // 2
    source_of, taker = tallies[1:1 + 2 * couples:2], tallies[2:2 + 2 * couples:2]
    slack = jnp.minimum(source_of - 1, reach - taker)
    moved = jax.random.randint(jax.random.fold_in(rng, 1), (couples,), 0, 1 << 20) % (slack + 1)
    tallies = tallies.at[1:1 + 2 * couples:2].set(source_of - moved).at[2:2 + 2 * couples:2].set(taker + moved)
    return tallies[jax.random.permutation(jax.random.fold_in(rng, 2), number_of)]


def normal_values(own_key, extent, deviation, reach, pieces=(), kind=jnp.bfloat16):
    entries = deviation * jax.random.normal(own_key, extent, jnp.float32)
    if pieces:
        entries = entries * block_scale(own_key, extent, pieces, -0.22, 0.18)
    return jnp.clip(entries, -reach, reach).astype(kind)


def setup_inputs(seed: int = 0, part: int = 0) -> dict:
    seeds = jax.random.split(jax.random.key(seed), 13)
    part_keys = jax.random.split(jax.random.fold_in(seeds[12], part), 13)
    memory_hidden = normal_values(part_keys[0], (MROWS, D), 1.0, 6.0, ((0, 4), (1, 4)))
    kv_weight = normal_values(seeds[1], (2, D, KVH * HD), D ** -0.5, 0.078125, ((2, 4),))
    kv_bias = normal_values(seeds[2], (2, KVH * HD), 0.5, 3.0, ((1, 4),))
    memory_sections = jnp.searchsorted(jnp.cumsum(ragged_sizes(part_keys[3], SECTIONS, MROWS, MROWS // 2, 0)), jnp.arange(MROWS), side="right").astype(jnp.int32)
    group_sections = plant(jax.random.randint(part_keys[4], (GROUPS,), 0, SECTIONS), jax.random.fold_in(part_keys[4], 1), 0, SECTIONS - 1).astype(jnp.int32)
    queries = draw_queries(jax.random.fold_in(jax.random.fold_in(seeds[12], part), 71), part)
    new_keys = normal_values(part_keys[6], (ROWS, KVH * HD), 1.0, 5.0, ((0, 4), (1, 4)))
    new_values = normal_values(part_keys[7], (ROWS, KVH * HD), 1.0, 5.0, ((0, 4), (1, 4)))
    cache_keys = draw_cache_keys(jax.random.fold_in(jax.random.fold_in(seeds[12], part), 71), part)
    cache_values = normal_values(part_keys[9], (REQUESTS, LMAX, KVH * HD), 1.0, 5.0, ((0, 4), (2, 4)))
    cache_lengths = draw_cache_lengths(jax.random.fold_in(jax.random.fold_in(seeds[12], part), 71), part)
    out_weight = normal_values(seeds[11], (HQ * HD, D), (HQ * HD // 256) ** -0.5, 1.25, ((0, 4), (1, 4)))
    return dict(memory_hidden=memory_hidden, kv_weight=kv_weight, kv_bias=kv_bias, memory_sections=memory_sections, group_sections=group_sections, queries=queries, new_keys=new_keys, new_values=new_values, cache_keys=cache_keys, cache_values=cache_values, cache_lengths=cache_lengths, out_weight=out_weight)


masked_score = -1e+30

def reference(memory_hidden, kv_weight, kv_bias, memory_sections, group_sections, queries, new_keys, new_values, cache_keys, cache_values, cache_lengths, out_weight):
    wide = memory_hidden.astype(jnp.float32)
    scale = lax.rsqrt(lax.optimization_barrier(jnp.mean(wide * wide, axis=1, keepdims=True)) + 1e-06)
    bias = kv_bias.astype(jnp.float32)
    mem_keys = (jnp.dot(memory_hidden, kv_weight[0], preferred_element_type=jnp.float32) * scale + bias[0]).astype(jnp.bfloat16)
    mem_values = (jnp.dot(memory_hidden, kv_weight[1], preferred_element_type=jnp.float32) * scale + bias[1]).astype(jnp.bfloat16)
    requests = cache_lengths.shape[0]
    per_head = HQ // KVH
    inv = 1.0 / HD ** 0.5
    query = queries.astype(jnp.float32).reshape(requests, NEW, KVH, per_head, HD)
    mk = mem_keys.astype(jnp.float32).reshape(MROWS, KVH, HD)
    mv = mem_values.astype(jnp.float32).reshape(MROWS, KVH, HD)
    ck = cache_keys.astype(jnp.float32).reshape(requests, LMAX, KVH, HD)
    cv = cache_values.astype(jnp.float32).reshape(requests, LMAX, KVH, HD)
    nk = new_keys.astype(jnp.float32).reshape(requests, NEW, KVH, HD)
    nv = new_values.astype(jnp.float32).reshape(requests, NEW, KVH, HD)
    sec_req = jnp.repeat(group_sections, REQ_DEV)
    mem_ok = (memory_sections[None, :] == sec_req[:, None])[:, None, None, None, :]
    cache_ok = (jnp.arange(LMAX)[None, :] < cache_lengths[:, None])[:, None, None, None, :]
    new_ok = (jnp.arange(NEW)[None, :] <= jnp.arange(NEW)[:, None])[None, :, None, None, :]
    s_mem = jnp.where(mem_ok, jnp.einsum('rnkgd,mkd->rnkgm', query, mk) * inv, masked_score)
    s_cache = jnp.where(cache_ok, jnp.einsum('rnkgd,rlkd->rnkgl', query, ck) * inv, masked_score)
    s_new = jnp.where(new_ok, jnp.einsum('rnkgd,rjkd->rnkgj', query, nk) * inv, masked_score)
    top = jnp.maximum(jnp.maximum(lax.optimization_barrier(jnp.max(s_mem, axis=-1)), lax.optimization_barrier(jnp.max(s_cache, axis=-1))), lax.optimization_barrier(jnp.max(s_new, axis=-1)))
    p_mem = jnp.where(mem_ok, jnp.exp(s_mem - top[..., None]), 0.0)
    p_cache = jnp.where(cache_ok, jnp.exp(s_cache - top[..., None]), 0.0)
    p_new = jnp.where(new_ok, jnp.exp(s_new - top[..., None]), 0.0)
    total = lax.optimization_barrier(jnp.sum(p_mem, axis=-1)) + lax.optimization_barrier(jnp.sum(p_cache, axis=-1)) + lax.optimization_barrier(jnp.sum(p_new, axis=-1))
    r_mem = lax.optimization_barrier(p_mem.astype(jnp.bfloat16)).astype(jnp.float32)
    r_cache = lax.optimization_barrier(p_cache.astype(jnp.bfloat16)).astype(jnp.float32)
    r_new = lax.optimization_barrier(p_new.astype(jnp.bfloat16)).astype(jnp.float32)
    acc = jnp.einsum('rnkgm,mkd->rnkgd', r_mem, mv)
    acc = acc + jnp.einsum('rnkgl,rlkd->rnkgd', r_cache, cv)
    acc = acc + jnp.einsum('rnkgj,rjkd->rnkgd', r_new, nv)
    attended = (acc / total[..., None]).astype(jnp.bfloat16).reshape(requests * NEW, HQ * HD)
    return jnp.dot(attended, out_weight, preferred_element_type=jnp.float32).astype(jnp.bfloat16)
```

```python
import functools

import jax
import jax.numpy as jnp
from jax import lax
from jax.experimental import pallas as pl
from jax.experimental.pallas import tpu as pltpu
from jax.sharding import PartitionSpec as P

D = 5120
HQ = 40
KVH = 8
HD = 128
NEW = 2
LMAX = 512
PER = HQ // KVH
INV = 1.0 / HD**0.5
MASKED = -1e30
MESH = pl.DeviceIdType.MESH
F32 = jnp.float32
BF16 = jnp.bfloat16


def up(n, m):
    return -(-n // m) * m


def nt(a, b):
    return lax.dot_general(a, b, (((1,), (1,)), ((), ())), preferred_element_type=F32)


def tn(a, b):
    return lax.dot_general(a, b, (((0,), (0,)), ((), ())), preferred_element_type=F32)


def nn(a, b):
    return lax.dot_general(a, b, (((1,), (0,)), ((), ())), preferred_element_type=F32)


def kernel(
    tp,
    dp,
    lens,
    group,
    hidden_h,
    kvw_h,
    bias_h,
    sections_h,
    q_h,
    nk_h,
    nv_h,
    ck_h,
    cv_h,
    wo_h,
    out,
    hid,
    kvw,
    bias,
    sections,
    q_v,
    nk,
    nv,
    ck,
    cv,
    wo,
    qm,
    acc_s,
    acc_r,
    st_s,
    st_r,
    att,
    osum_s,
    osum_r,
    load_sem,
    hid_ss,
    hid_rs,
    q_ss,
    q_rs,
    acc_ss,
    acc_rs,
    st_ss,
    st_rs,
    att_ss,
    att_rs,
    o_ss,
    o_rs,
):
    t = lax.axis_index("tp")
    d = lax.axis_index("dp")
    mdev, feat = hid.shape[1], hid.shape[2]
    rows, heads = q_v.shape[0], kvw.shape[2] // HD
    requests = ck.shape[0]
    qr = PER * rows
    qp = qm.shape[2]

    def at_tp(off):
        return {"tp": lax.rem(t + off, tp)}

    def at_dp(off):
        return {"dp": lax.rem(d + off + dp, dp)}

    pairs = (
        (q_h, q_v),
        (hidden_h, hid.at[0]),
        (nk_h, nk),
        (nv_h, nv),
        (bias_h, bias),
        (sections_h, sections),
        (ck_h, ck),
        (cv_h, cv),
        (kvw_h, kvw),
        (wo_h, wo),
    )
    loads = [pltpu.make_async_copy(s, v, load_sem.at[i]) for i, (s, v) in enumerate(pairs)]
    for copy in loads:
        copy.start()
    l_q, l_hid, l_nk, l_nv, l_bias, l_sec, l_ck, l_cv, l_kvw, l_wo = loads

    barrier = pltpu.get_barrier_semaphore()
    for off in range(1, tp):
        pl.semaphore_signal(barrier, inc=1, device_id=at_tp(off), device_id_type=MESH)
    for off in range(1, dp):
        pl.semaphore_signal(barrier, inc=1, device_id=at_dp(off), device_id_type=MESH)

    l_q.wait()
    q_wide = q_v[...].astype(F32)
    section_rows = jnp.full((qp - qr, HD), group[0], F32)
    for k in range(heads):
        parts = [q_wide[:, (k * PER + g) * HD : (k * PER + g + 1) * HD] for g in range(PER)]
        qm[0, k] = jnp.concatenate(parts + [section_rows], axis=0).astype(BF16)
    st_s[...] = jnp.zeros_like(st_s)

    l_hid.wait()
    pl.semaphore_wait(barrier, tp - 1 + dp - 1)

    def send(src, dst, ss, rs, to):
        copy = pltpu.make_async_remote_copy(
            src_ref=src, dst_ref=dst, send_sem=ss, recv_sem=rs, device_id=to, device_id_type=MESH
        )
        copy.start()
        return copy

    hid_c = [None] * tp
    for off in range(1, tp):
        hid_c[off] = send(hid.at[0], hid.at[off], hid_ss.at[off], hid_rs.at[off], at_tp(off))
    q_c = [None] * dp
    for off in range(1, dp):
        q_c[off] = send(qm.at[0], qm.at[off], q_ss.at[off], q_rs.at[off], at_dp(off))

    for copy in (l_nk, l_nv, l_ck, l_cv, l_bias, l_sec):
        copy.wait()
    row = lax.broadcasted_iota(jnp.int32, (qr, 1), 0)
    token = lax.rem(row, rows)
    request = lax.div(token, NEW)
    slot = lax.broadcasted_iota(jnp.int32, (1, LMAX), 1)
    fresh = lax.broadcasted_iota(jnp.int32, (1, rows), 1)
    new_ok = (lax.div(fresh, NEW) == request) & (fresh <= token)
    own = []
    for k in range(heads):
        cols = slice(k * HD, (k + 1) * HD)
        qk = qm[0, k][:qr]
        scores = [jnp.where(new_ok, nt(qk, nk[:, cols]) * INV, MASKED)]
        for r in range(requests):
            ok = (request == r) & (slot < lens[r])
            scores.append(jnp.where(ok, nt(qk, ck[r, :, cols]) * INV, MASKED))
        top = functools.reduce(
            jnp.maximum, [jnp.max(s, axis=1, keepdims=True) for s in scores]
        )
        weights = [jnp.exp(s - top) for s in scores]
        total = functools.reduce(jnp.add, [jnp.sum(p, axis=1, keepdims=True) for p in weights])
        acc = nn(weights[0].astype(BF16), nv[:, cols])
        for r in range(requests):
            acc = acc + nn(weights[r + 1].astype(BF16), cv[r, :, cols])
        own.append((top, total, acc))

    l_kvw.wait()
    proj = [jnp.zeros((mdev, heads * HD), F32) for _ in range(2)]
    squares = jnp.zeros((mdev, 1), F32)
    for off in range(tp):
        if off:
            hid_c[off].wait_recv()
        piece = hid[off]
        wide = piece.astype(F32)
        squares = squares + jnp.sum(wide * wide, axis=1, keepdims=True)
        first = pl.multiple_of(lax.rem(t - off + tp, tp) * feat, feat)
        for s in range(2):
            proj[s] = proj[s] + nn(piece, kvw[s, pl.ds(first, feat), :])
    scale = lax.rsqrt(squares / D + 1e-06)
    mem_k, mem_v = [
        (proj[s] * scale + bias[s : s + 1, :].astype(F32)).astype(BF16) for s in range(2)
    ]

    mrows = sections.shape[1]
    lane = lax.broadcasted_iota(jnp.int32, (mdev, mrows), 1)
    place = lax.broadcasted_iota(jnp.int32, (mdev, mrows), 0) + d * mdev
    mine = jnp.where(lane == place, sections[...].astype(F32), 0.0)
    section = jnp.sum(mine, axis=1, keepdims=True)
    acc_c = [None] * dp
    st_c = [None] * dp
    for off in list(range(1, dp)) + [0]:
        if off:
            q_c[off].wait_recv()
        for k in range(heads):
            cols = slice(k * HD, (k + 1) * HD)
            qk = qm[off, k]
            ok = section == qk[qr : qr + 1, 0:1].astype(F32)
            s = jnp.where(ok, nt(mem_k[:, cols], qk) * INV, MASKED)
            top = jnp.max(s, axis=0, keepdims=True)
            p = jnp.where(ok, jnp.exp(s - top), 0.0)
            acc_s[off, k] = tn(p.astype(BF16), mem_v[:, cols]).astype(BF16)
            st_s[off, 2 * k : 2 * k + 1, 0:qp] = top
            st_s[off, 2 * k + 1 : 2 * k + 2, 0:qp] = jnp.sum(p, axis=0, keepdims=True)
        if off:
            st_c[off] = send(st_s.at[off], st_r.at[off], st_ss.at[off], st_rs.at[off], at_dp(-off))
            acc_c[off] = send(
                acc_s.at[off], acc_r.at[off], acc_ss.at[off], acc_rs.at[off], at_dp(-off)
            )

    for off in range(1, dp):
        st_c[off].wait_recv()
        acc_c[off].wait_recv()
    stats = [jnp.transpose((st_r if off else st_s)[off]) for off in range(dp)]
    blocks = []
    for k in range(heads):
        top_c, total_c, acc = own[k]
        tops = [st[:qr, 2 * k : 2 * k + 1] for st in stats]
        totals = [st[:qr, 2 * k + 1 : 2 * k + 2] for st in stats]
        top = functools.reduce(jnp.maximum, tops, top_c)
        factor = jnp.exp(top_c - top)
        total = total_c * factor
        acc = acc * factor
        for off in range(dp):
            factor = jnp.exp(tops[off] - top)
            total = total + totals[off] * factor
            acc = acc + (acc_r if off else acc_s)[off, k][:qr].astype(F32) * factor
        blocks.append(acc / total)
    ar = att.shape[1]
    if ar > heads * qr:
        blocks.append(jnp.zeros((ar - heads * qr, HD), F32))
    att[0] = jnp.concatenate(blocks, axis=0).astype(BF16)
    att_c = [None] * dp
    for off in range(1, dp):
        att_c[off] = send(att.at[0], att.at[off], att_ss.at[off], att_rs.at[off], at_dp(off))

    l_wo.wait()
    for off in range(1, dp):
        att_c[off].wait_recv()
    groups = []
    for g in range(dp):
        a = att[lax.rem(d - g + dp, dp)].astype(F32)
        groups.append(
            jnp.concatenate([a[h * rows : (h + 1) * rows] for h in range(heads * PER)], axis=1)
        )
    lhs = jnp.concatenate(groups, axis=0).astype(BF16)
    orows = osum_s.shape[1]
    result = nn(lhs, wo[...])
    for i in range(tp):
        osum_s[i] = result[i * orows : (i + 1) * orows]
    o_c = [None] * tp
    for off in range(1, tp):
        to = lax.rem(t + off, tp)
        o_c[off] = send(osum_s.at[to], osum_r.at[off], o_ss.at[off], o_rs.at[off], at_tp(off))
    summed = osum_s[t]
    for off in range(1, tp):
        o_c[off].wait_recv()
        summed = summed + osum_r[off]
    out[...] = summed.astype(BF16)

    for copies in (hid_c, q_c, st_c, acc_c, att_c, o_c):
        for copy in copies:
            if copy is not None:
                copy.wait_send()


def body(
    tp,
    dp,
    memory_hidden,
    kv_weight,
    kv_bias,
    memory_sections,
    group_sections,
    queries,
    new_keys,
    new_values,
    cache_keys,
    cache_values,
    cache_lengths,
    out_weight,
):
    mdev, feat = memory_hidden.shape
    heads = kv_weight.shape[2] // HD
    rows = queries.shape[0]
    qp = up(PER * rows + 1, 16)
    ar = up(heads * PER * rows, 16)
    ocols = out_weight.shape[1]
    orows = dp * rows // tp
    any_spec = pl.BlockSpec(memory_space=pl.ANY)
    smem = pl.BlockSpec(memory_space=pltpu.SMEM)
    dma = pltpu.SemaphoreType.DMA
    like = lambda a: pltpu.VMEM(a.shape, a.dtype)
    sections = memory_sections.reshape(1, -1)
    return pl.pallas_call(
        functools.partial(kernel, tp, dp),
        out_shape=jax.ShapeDtypeStruct((orows, ocols), BF16),
        in_specs=[smem, smem] + [any_spec] * 10,
        out_specs=pl.BlockSpec(memory_space=pltpu.VMEM),
        scratch_shapes=[
            pltpu.VMEM((tp, mdev, feat), BF16),
            like(kv_weight),
            like(kv_bias),
            like(sections),
            like(queries),
            like(new_keys),
            like(new_values),
            like(cache_keys),
            like(cache_values),
            like(out_weight),
            pltpu.VMEM((dp, heads, qp, HD), BF16),
            pltpu.VMEM((dp, heads, qp, HD), BF16),
            pltpu.VMEM((dp, heads, qp, HD), BF16),
            pltpu.VMEM((dp, 8, HD), F32),
            pltpu.VMEM((dp, 8, HD), F32),
            pltpu.VMEM((dp, ar, HD), BF16),
            pltpu.VMEM((tp, orows, ocols), F32),
            pltpu.VMEM((tp, orows, ocols), F32),
            dma((10,)),
            dma((tp,)),
            dma((tp,)),
        ]
        + [dma((dp,))] * 8
        + [dma((tp,))] * 2,
        compiler_params=pltpu.CompilerParams(
            collective_id=0, has_side_effects=True, vmem_limit_bytes=48 * 1024 * 1024
        ),
        name="decode_step",
    )(
        cache_lengths,
        group_sections,
        memory_hidden,
        kv_weight,
        kv_bias,
        sections,
        queries,
        new_keys,
        new_values,
        cache_keys,
        cache_values,
        out_weight,
    )


def solution(mesh):
    return jax.shard_map(
        functools.partial(body, mesh.shape["tp"], mesh.shape["dp"]),
        mesh=mesh,
        in_specs=(
            P(("parts", "dp"), "tp"),
            P(None, None, "tp"),
            P(None, "tp"),
            P("parts"),
            P(("parts", "dp")),
            P(("parts", "dp"), "tp"),
            P(("parts", "dp"), "tp"),
            P(("parts", "dp"), "tp"),
            P(("parts", "dp"), None, "tp"),
            P(("parts", "dp"), None, "tp"),
            P(("parts", "dp")),
            P("tp", "dp"),
        ),
        out_specs=P(("parts", "tp"), "dp"),
        check_vma=False,
    )
```

```python
import functools

import jax
import jax.numpy as jnp
from jax import lax
from jax.experimental import pallas as pl
from jax.experimental.pallas import tpu as pltpu
from jax.sharding import PartitionSpec as P

D = 5120
HQ = 40
KVH = 8
HD = 128
NEW = 2
LMAX = 512
PER = HQ // KVH
INV = 1.0 / HD**0.5
MASKED = -1e30
MESH = pl.DeviceIdType.MESH
F32 = jnp.float32
BF16 = jnp.bfloat16


def up(n, m):
    return -(-n // m) * m


def nt(a, b):
    return lax.dot_general(a, b, (((1,), (1,)), ((), ())), preferred_element_type=F32)


def tn(a, b):
    return lax.dot_general(a, b, (((0,), (0,)), ((), ())), preferred_element_type=F32)


def nn(a, b):
    return lax.dot_general(a, b, (((1,), (0,)), ((), ())), preferred_element_type=F32)


def kernel(
    tp,
    dp,
    lens,
    group,
    hidden_h,
    kvw_h,
    bias_h,
    sections_h,
    q_h,
    nk_h,
    nv_h,
    ck_h,
    cv_h,
    wo_h,
    out,
    hid,
    kvw,
    bias,
    sections,
    q_v,
    nk,
    nv,
    ck,
    cv,
    wo,
    qm,
    acc_s,
    acc_r,
    st_s,
    st_r,
    att,
    osum_s,
    osum_r,
    load_sem,
    hid_ss,
    hid_rs,
    q_ss,
    q_rs,
    acc_ss,
    acc_rs,
    st_ss,
    st_rs,
    att_ss,
    att_rs,
    o_ss,
    o_rs,
):
    t = lax.axis_index("tp")
    d = lax.axis_index("dp")
    mdev, feat = hid.shape[1], hid.shape[2]
    rows, heads = q_v.shape[0], kvw.shape[2] // HD
    requests = ck.shape[0]
    qr = PER * rows
    qp = qm.shape[2]

    def at_tp(off):
        return {"tp": lax.rem(t + off, tp)}

    def at_dp(off):
        return {"dp": lax.rem(d + off + dp, dp)}

    pairs = (
        (q_h, q_v),
        (hidden_h, hid.at[0]),
        (nk_h, nk),
        (nv_h, nv),
        (bias_h, bias),
        (sections_h, sections),
        (ck_h, ck),
        (cv_h, cv),
        (kvw_h, kvw),
        (wo_h, wo),
    )
    loads = [pltpu.make_async_copy(s, v, load_sem.at[i]) for i, (s, v) in enumerate(pairs)]
    for copy in loads:
        copy.start()
    l_q, l_hid, l_nk, l_nv, l_bias, l_sec, l_ck, l_cv, l_kvw, l_wo = loads

    barrier = pltpu.get_barrier_semaphore()
    for off in range(1, tp):
        pl.semaphore_signal(barrier, inc=1, device_id=at_tp(off), device_id_type=MESH)
    for off in range(1, dp):
        pl.semaphore_signal(barrier, inc=1, device_id=at_dp(off), device_id_type=MESH)

    l_q.wait()
    q_wide = q_v[...].astype(F32)
    section_rows = jnp.full((qp - qr, HD), group[0], F32)
    for k in range(heads):
        parts = [q_wide[:, (k * PER + g) * HD : (k * PER + g + 1) * HD] for g in range(PER)]
        qm[0, k] = jnp.concatenate(parts + [section_rows], axis=0).astype(BF16)
    st_s[...] = jnp.zeros_like(st_s)

    l_hid.wait()
    pl.semaphore_wait(barrier, tp - 1 + dp - 1)

    def send(src, dst, ss, rs, to):
        copy = pltpu.make_async_remote_copy(
            src_ref=src, dst_ref=dst, send_sem=ss, recv_sem=rs, device_id=to, device_id_type=MESH
        )
        copy.start()
        return copy

    hid_c = [None] * tp
    for off in range(1, tp):
        hid_c[off] = send(hid.at[0], hid.at[off], hid_ss.at[off], hid_rs.at[off], at_tp(off))
    q_c = [None] * dp
    for off in range(1, dp):
        q_c[off] = send(qm.at[0], qm.at[off], q_ss.at[off], q_rs.at[off], at_dp(off))

    for copy in (l_nk, l_nv, l_ck, l_cv, l_bias, l_sec):
        copy.wait()
    row = lax.broadcasted_iota(jnp.int32, (qr, 1), 0)
    token = lax.rem(row, rows)
    request = lax.div(token, NEW)
    slot = lax.broadcasted_iota(jnp.int32, (1, LMAX), 1)
    fresh = lax.broadcasted_iota(jnp.int32, (1, rows), 1)
    new_ok = (lax.div(fresh, NEW) == request) & (fresh <= token)
    own = []
    for k in range(heads):
        cols = slice(k * HD, (k + 1) * HD)
        qk = qm[0, k][:qr]
        scores = [jnp.where(new_ok, nt(qk, nk[:, cols]) * INV, MASKED)]
        for r in range(requests):
            ok = (request == r) & (slot < lens[r])
            scores.append(jnp.where(ok, nt(qk, ck[r, :, cols]) * INV, MASKED))
        top = functools.reduce(
            jnp.maximum, [jnp.max(s, axis=1, keepdims=True) for s in scores]
        )
        weights = [jnp.exp(s - top) for s in scores]
        total = functools.reduce(jnp.add, [jnp.sum(p, axis=1, keepdims=True) for p in weights])
        acc = nn(weights[0].astype(BF16), nv[:, cols])
        for r in range(requests):
            acc = acc + nn(weights[r + 1].astype(BF16), cv[r, :, cols])
        own.append((top, total, acc))

    l_kvw.wait()
    proj = [jnp.zeros((mdev, heads * HD), F32) for _ in range(2)]
    squares = jnp.zeros((mdev, 1), F32)
    for off in range(tp):
        if off:
            hid_c[off].wait_recv()
        piece = hid[off]
        wide = piece.astype(F32)
        squares = squares + jnp.sum(wide * wide, axis=1, keepdims=True)
        first = pl.multiple_of(lax.rem(t - off + tp, tp) * feat, feat)
        for s in range(2):
            proj[s] = proj[s] + nn(piece, kvw[s, pl.ds(first, feat), :])
    scale = lax.rsqrt(squares / D + 1e-06)
    mem_k, mem_v = [
        (proj[s] * scale + bias[s : s + 1, :].astype(F32)).astype(BF16) for s in range(2)
    ]

    mrows = sections.shape[1]
    lane = lax.broadcasted_iota(jnp.int32, (mdev, mrows), 1)
    place = lax.broadcasted_iota(jnp.int32, (mdev, mrows), 0) + d * mdev
    mine = jnp.where(lane == place, sections[...].astype(F32), 0.0)
    section = jnp.sum(mine, axis=1, keepdims=True)
    acc_c = [None] * dp
    st_c = [None] * dp
    for off in list(range(1, dp)) + [0]:
        if off:
            q_c[off].wait_recv()
        for k in range(heads):
            cols = slice(k * HD, (k + 1) * HD)
            qk = qm[off, k]
            ok = section == qk[qr : qr + 1, 0:1].astype(F32)
            s = jnp.where(ok, nt(mem_k[:, cols], qk) * INV, MASKED)
            top = jnp.max(s, axis=0, keepdims=True)
            p = jnp.where(ok, jnp.exp(s - top), 0.0)
            acc_s[off, k] = tn(p.astype(BF16), mem_v[:, cols]).astype(BF16)
            st_s[off, 2 * k : 2 * k + 1, 0:qp] = top
            st_s[off, 2 * k + 1 : 2 * k + 2, 0:qp] = jnp.sum(p, axis=0, keepdims=True)
        if off:
            st_c[off] = send(st_s.at[off], st_r.at[off], st_ss.at[off], st_rs.at[off], at_dp(-off))
            acc_c[off] = send(
                acc_s.at[off], acc_r.at[off], acc_ss.at[off], acc_rs.at[off], at_dp(-off)
            )

    for off in range(1, dp):
        st_c[off].wait_recv()
        acc_c[off].wait_recv()
    stats = [jnp.transpose((st_r if off else st_s)[off]) for off in range(dp)]
    blocks = []
    for k in range(heads):
        top_c, total_c, acc = own[k]
        tops = [st[:qr, 2 * k : 2 * k + 1] for st in stats]
        totals = [st[:qr, 2 * k + 1 : 2 * k + 2] for st in stats]
        top = functools.reduce(jnp.maximum, tops, top_c)
        factor = jnp.exp(top_c - top)
        total = total_c * factor
        acc = acc * factor
        for off in range(dp):
            factor = jnp.exp(tops[off] - top)
            total = total + totals[off] * factor
            acc = acc + (acc_r if off else acc_s)[off, k][:qr].astype(F32) * factor
        blocks.append(acc / total)
    ar = att.shape[1]
    if ar > heads * qr:
        blocks.append(jnp.zeros((ar - heads * qr, HD), F32))
    att[0] = jnp.concatenate(blocks, axis=0).astype(BF16)
    att_c = [None] * dp
    for off in range(1, dp):
        att_c[off] = send(att.at[0], att.at[off], att_ss.at[off], att_rs.at[off], at_dp(off))

    l_wo.wait()
    for off in range(1, dp):
        att_c[off].wait_recv()
    groups = []
    for g in range(dp):
        a = att[lax.rem(d - g + dp, dp)].astype(F32)
        groups.append(
            jnp.concatenate([a[h * rows : (h + 1) * rows] for h in range(heads * PER)], axis=1)
        )
    lhs = jnp.concatenate(groups, axis=0).astype(BF16)
    orows = osum_s.shape[1]
    result = nn(lhs, wo[...])
    for i in range(tp):
        osum_s[i] = result[i * orows : (i + 1) * orows]
    o_c = [None] * tp
    for off in range(1, tp):
        to = lax.rem(t + off, tp)
        o_c[off] = send(osum_s.at[to], osum_r.at[off], o_ss.at[off], o_rs.at[off], at_tp(off))
    summed = osum_s[t]
    for off in range(1, tp):
        o_c[off].wait_recv()
        summed = summed + osum_r[off]
    out[...] = summed.astype(BF16)

    for copies in (hid_c, q_c, st_c, acc_c, att_c, o_c):
        for copy in copies:
            if copy is not None:
                copy.wait_send()


def body(
    tp,
    dp,
    memory_hidden,
    kv_weight,
    kv_bias,
    memory_sections,
    group_sections,
    queries,
    new_keys,
    new_values,
    cache_keys,
    cache_values,
    cache_lengths,
    out_weight,
):
    mdev, feat = memory_hidden.shape
    heads = kv_weight.shape[2] // HD
    rows = queries.shape[0]
    qp = up(PER * rows + 1, 16)
    ar = up(heads * PER * rows, 16)
    ocols = out_weight.shape[1]
    orows = dp * rows // tp
    any_spec = pl.BlockSpec(memory_space=pl.ANY)
    smem = pl.BlockSpec(memory_space=pltpu.SMEM)
    dma = pltpu.SemaphoreType.DMA
    like = lambda a: pltpu.VMEM(a.shape, a.dtype)
    sections = memory_sections.reshape(1, -1)
    return pl.pallas_call(
        functools.partial(kernel, tp, dp),
        out_shape=jax.ShapeDtypeStruct((orows, ocols), BF16),
        in_specs=[smem, smem] + [any_spec] * 10,
        out_specs=pl.BlockSpec(memory_space=pltpu.VMEM),
        scratch_shapes=[
            pltpu.VMEM((tp, mdev, feat), BF16),
            like(kv_weight),
            like(kv_bias),
            like(sections),
            like(queries),
            like(new_keys),
            like(new_values),
            like(cache_keys),
            like(cache_values),
            like(out_weight),
            pltpu.VMEM((dp, heads, qp, HD), BF16),
            pltpu.VMEM((dp, heads, qp, HD), BF16),
            pltpu.VMEM((dp, heads, qp, HD), BF16),
            pltpu.VMEM((dp, 8, HD), F32),
            pltpu.VMEM((dp, 8, HD), F32),
            pltpu.VMEM((dp, ar, HD), BF16),
            pltpu.VMEM((tp, orows, ocols), F32),
            pltpu.VMEM((tp, orows, ocols), F32),
            dma((10,)),
            dma((tp,)),
            dma((tp,)),
        ]
        + [dma((dp,))] * 8
        + [dma((tp,))] * 2,
        compiler_params=pltpu.CompilerParams(
            collective_id=0, has_side_effects=True, vmem_limit_bytes=63 * 1024 * 1024
        ),
        name="decode_step",
    )(
        cache_lengths,
        group_sections,
        memory_hidden,
        kv_weight,
        kv_bias,
        sections,
        queries,
        new_keys,
        new_values,
        cache_keys,
        cache_values,
        out_weight,
    )


def solution(mesh):
    return jax.shard_map(
        functools.partial(body, mesh.shape["tp"], mesh.shape["dp"]),
        mesh=mesh,
        in_specs=(
            P(("parts", "dp"), "tp"),
            P(None, None, "tp"),
            P(None, "tp"),
            P("parts"),
            P(("parts", "dp")),
            P(("parts", "dp"), "tp"),
            P(("parts", "dp"), "tp"),
            P(("parts", "dp"), "tp"),
            P(("parts", "dp"), None, "tp"),
            P(("parts", "dp"), None, "tp"),
            P(("parts", "dp")),
            P("tp", "dp"),
        ),
        out_specs=P(("parts", "tp"), "dp"),
        check_vma=False,
    )
```

```python
import functools

import jax
import jax.numpy as jnp
from jax import lax
from jax.experimental import pallas as pl
from jax.experimental.pallas import tpu as pltpu
from jax.sharding import PartitionSpec as P

D = 5120
HQ = 40
KVH = 8
HD = 128
NEW = 2
LMAX = 512
PER = HQ // KVH
INV = 1.0 / HD**0.5
MASKED = -1e30
MESH = pl.DeviceIdType.MESH
F32 = jnp.float32
BF16 = jnp.bfloat16


def up(n, m):
    return -(-n // m) * m


def nt(a, b):
    return lax.dot_general(a, b, (((1,), (1,)), ((), ())), preferred_element_type=F32)


def tn(a, b):
    return lax.dot_general(a, b, (((0,), (0,)), ((), ())), preferred_element_type=F32)


def nn(a, b):
    return lax.dot_general(a, b, (((1,), (0,)), ((), ())), preferred_element_type=F32)


def kernel(
    tp,
    dp,
    lens,
    group,
    hidden_h,
    kvw_h,
    bias_h,
    sections_h,
    q_h,
    nk_h,
    nv_h,
    ck_h,
    cv_h,
    wo_h,
    out,
    hid,
    kvw,
    bias,
    sections,
    q_v,
    nk,
    nv,
    ck,
    cv,
    wo,
    qm,
    acc_s,
    acc_r,
    st_s,
    st_r,
    att,
    osum,
    osum_s,
    osum_r,
    load_sem,
    hid_ss,
    hid_rs,
    q_ss,
    q_rs,
    acc_ss,
    acc_rs,
    st_ss,
    st_rs,
    att_ss,
    att_rs,
    o_ss,
    o_rs,
):
    t = lax.axis_index("tp")
    d = lax.axis_index("dp")
    chunks, mdev, width = hid.shape[1:]
    feat = chunks * width
    relay = tp == 4
    rows, heads = q_v.shape[0], kvw.shape[2] // HD
    requests = ck.shape[0]
    qr = PER * rows
    qp = qm.shape[2]

    def at_tp(off):
        return {"tp": lax.rem(t + off, tp)}

    def at_dp(off):
        return {"dp": lax.rem(d + off + dp, dp)}

    pairs = (
        (q_h, q_v),
        (nk_h, nk),
        (nv_h, nv),
        (bias_h, bias),
        (sections_h, sections),
        (ck_h, ck),
        (cv_h, cv),
        (kvw_h, kvw),
        (wo_h, wo),
    ) + tuple(
        (hidden_h.at[:, c * width : (c + 1) * width], hid.at[0, c]) for c in range(chunks)
    )
    loads = [pltpu.make_async_copy(s, v, load_sem.at[i]) for i, (s, v) in enumerate(pairs)]
    for copy in loads:
        copy.start()
    l_q, l_nk, l_nv, l_bias, l_sec, l_ck, l_cv, l_kvw, l_wo = loads[:9]

    barrier = pltpu.get_barrier_semaphore()
    for off in range(1, tp):
        pl.semaphore_signal(barrier, inc=1, device_id=at_tp(off), device_id_type=MESH)
    for off in range(1, dp):
        pl.semaphore_signal(barrier, inc=1, device_id=at_dp(off), device_id_type=MESH)

    pl.semaphore_wait(barrier, tp - 1 + dp - 1)

    def send(src, dst, ss, rs, to):
        copy = pltpu.make_async_remote_copy(
            src_ref=src, dst_ref=dst, send_sem=ss, recv_sem=rs, device_id=to, device_id_type=MESH
        )
        copy.start()
        return copy

    if relay:
        source = [t, t + 1 - 2 * lax.rem(t, 2), lax.rem(t + 2, tp), tp - 1 - t]
        direct = {2: source[2], 1: source[1]}
    else:
        source = [lax.rem(t - off + tp, tp) for off in range(tp)]
        direct = {off: lax.rem(t + off, tp) for off in range(1, tp)}
    hid_c = [[None] * chunks for _ in range(tp)]

    def send_hidden(slot, c, src, to):
        hid_c[slot][c] = send(
            src, hid.at[slot, c], hid_ss.at[slot, c], hid_rs.at[slot, c], {"tp": to}
        )

    def hand_on(c):
        if relay:
            hid_c[2][c].wait_recv()
            send_hidden(3, c, hid.at[2, c], source[1])

    for slot, to in direct.items():
        for c in range(chunks):
            send_hidden(slot, c, hidden_h.at[:, c * width : (c + 1) * width], to)

    l_q.wait()
    q_wide = q_v[...].astype(F32)
    section_rows = jnp.full((qp - qr, HD), group[0], F32)
    for k in range(heads):
        parts = [q_wide[:, (k * PER + g) * HD : (k * PER + g + 1) * HD] for g in range(PER)]
        qm[0, k] = jnp.concatenate(parts + [section_rows], axis=0).astype(BF16)
    st_s[...] = jnp.zeros_like(st_s)

    q_c = [None] * dp
    for off in range(1, dp):
        q_c[off] = send(qm.at[0], qm.at[off], q_ss.at[off], q_rs.at[off], at_dp(off))

    for copy in (l_nk, l_nv, l_ck, l_cv, l_bias, l_sec):
        copy.wait()
    row = lax.broadcasted_iota(jnp.int32, (qr, 1), 0)
    token = lax.rem(row, rows)
    request = lax.div(token, NEW)
    slot = lax.broadcasted_iota(jnp.int32, (1, LMAX), 1)
    fresh = lax.broadcasted_iota(jnp.int32, (1, rows), 1)
    new_ok = (lax.div(fresh, NEW) == request) & (fresh <= token)
    own = []
    for k in range(heads):
        cols = slice(k * HD, (k + 1) * HD)
        qk = qm[0, k][:qr]
        scores = [jnp.where(new_ok, nt(qk, nk[:, cols]) * INV, MASKED)]
        for r in range(requests):
            ok = (request == r) & (slot < lens[r])
            scores.append(jnp.where(ok, nt(qk, ck[r, :, cols]) * INV, MASKED))
        top = functools.reduce(
            jnp.maximum, [jnp.max(s, axis=1, keepdims=True) for s in scores]
        )
        weights = [jnp.exp(s - top) for s in scores]
        total = functools.reduce(jnp.add, [jnp.sum(p, axis=1, keepdims=True) for p in weights])
        acc = nn(weights[0].astype(BF16), nv[:, cols])
        for r in range(requests):
            acc = acc + nn(weights[r + 1].astype(BF16), cv[r, :, cols])
        own.append((top, total, acc))
        if k < chunks:
            hand_on(k)

    l_kvw.wait()
    proj = [jnp.zeros((mdev, heads * HD), F32) for _ in range(2)]
    squares = jnp.zeros((mdev, 1), F32)
    for copy in loads[9:]:
        copy.wait()
    handed = min(heads, chunks)
    for slot in range(tp):
        if relay and slot == 2:
            for c in range(handed, chunks):
                hand_on(c)
        for c in range(chunks):
            if slot and not (relay and slot == 2):
                hid_c[slot][c].wait_recv()
            piece = hid[slot, c]
            wide = piece.astype(F32)
            squares = squares + jnp.sum(wide * wide, axis=1, keepdims=True)
            first = pl.multiple_of(source[slot] * feat + c * width, width)
            for s in range(2):
                proj[s] = proj[s] + nn(piece, kvw[s, pl.ds(first, width), :])
    scale = lax.rsqrt(squares / D + 1e-06)
    mem_k, mem_v = [
        (proj[s] * scale + bias[s : s + 1, :].astype(F32)).astype(BF16) for s in range(2)
    ]

    mrows = sections.shape[1]
    lane = lax.broadcasted_iota(jnp.int32, (mdev, mrows), 1)
    place = lax.broadcasted_iota(jnp.int32, (mdev, mrows), 0) + d * mdev
    mine = jnp.where(lane == place, sections[...].astype(F32), 0.0)
    section = jnp.sum(mine, axis=1, keepdims=True)
    ar = att.shape[1]

    def pack(blocks):
        if ar > heads * qr:
            blocks = blocks + [jnp.zeros((ar - heads * qr, HD), F32)]
        return jnp.concatenate(blocks, axis=0).astype(BF16)

    acc_c = [None] * dp
    st_c = [None] * dp
    for off in list(range(1, dp)) + [0]:
        if off:
            q_c[off].wait_recv()
        sums = []
        for k in range(heads):
            cols = slice(k * HD, (k + 1) * HD)
            qk = qm[off, k]
            ok = section == qk[qr : qr + 1, 0:1].astype(F32)
            s = jnp.where(ok, nt(mem_k[:, cols], qk) * INV, MASKED)
            top = jnp.max(s, axis=0, keepdims=True)
            p = jnp.where(ok, jnp.exp(s - top), 0.0)
            sums.append(tn(p.astype(BF16), mem_v[:, cols])[:qr])
            st_s[off, 2 * k : 2 * k + 1, 0:qp] = top
            st_s[off, 2 * k + 1 : 2 * k + 2, 0:qp] = jnp.sum(p, axis=0, keepdims=True)
        acc_s[off] = pack(sums)
        if off:
            st_c[off] = send(st_s.at[off], st_r.at[off], st_ss.at[off], st_rs.at[off], at_dp(-off))
            acc_c[off] = send(
                acc_s.at[off], acc_r.at[off], acc_ss.at[off], acc_rs.at[off], at_dp(-off)
            )

    def merge(state, offs):
        stats = [jnp.transpose((st_r if off else st_s)[off]) for off in offs]
        terms = [(acc_r if off else acc_s)[off].astype(F32) for off in offs]
        merged = []
        for k in range(heads):
            top_c, total_c, acc = state[k]
            tops = [st[:qr, 2 * k : 2 * k + 1] for st in stats]
            top = functools.reduce(jnp.maximum, tops, top_c)
            factor = jnp.exp(top_c - top)
            total = total_c * factor
            acc = acc * factor
            for i in range(len(offs)):
                factor = jnp.exp(tops[i] - top)
                total = total + stats[i][:qr, 2 * k + 1 : 2 * k + 2] * factor
                acc = acc + terms[i][k * qr : (k + 1) * qr] * factor
            merged.append((top, total, acc))
        return merged

    own = merge(own, [0])
    for off in range(1, dp):
        st_c[off].wait_recv()
        acc_c[off].wait_recv()
    own = merge(own, list(range(1, dp)))
    att[0] = pack([acc / total for _, total, acc in own])
    att_c = [None] * dp
    for off in range(1, dp):
        att_c[off] = send(att.at[0], att.at[off], att_ss.at[off], att_rs.at[off], at_dp(off))

    l_wo.wait()
    for off in range(1, dp):
        att_c[off].wait_recv()
    groups = []
    for g in range(dp):
        a = att[lax.rem(d - g + dp, dp)].astype(F32)
        groups.append(
            jnp.concatenate([a[h * rows : (h + 1) * rows] for h in range(heads * PER)], axis=1)
        )
    lhs = jnp.concatenate(groups, axis=0).astype(BF16)
    orows, ocols = osum.shape[1:]
    cuts = osum_s.shape[1] // orows
    span = ocols // cuts
    result = nn(lhs, wo[...])
    for i in range(tp):
        mine = result[i * orows : (i + 1) * orows]
        osum[i] = mine
        osum_s[i] = jnp.concatenate(
            [mine[:, c * span : (c + 1) * span] for c in range(cuts)], axis=0
        ).astype(BF16)
    o_c = [None] * tp
    for off in range(1, tp):
        to = lax.rem(t + off, tp)
        o_c[off] = send(osum_s.at[to], osum_r.at[off], o_ss.at[off], o_rs.at[off], at_tp(off))
    own_sum = osum[t]
    summed = [own_sum[:, c * span : (c + 1) * span] for c in range(cuts)]
    for off in range(1, tp):
        o_c[off].wait_recv()
        came = osum_r[off].astype(F32)
        summed = [v + came[c * orows : (c + 1) * orows] for c, v in enumerate(summed)]
    out[...] = jnp.concatenate(summed, axis=1).astype(BF16)

    for copies in hid_c + [q_c, st_c, acc_c, att_c, o_c]:
        for copy in copies:
            if copy is not None:
                copy.wait_send()


def body(
    tp,
    dp,
    memory_hidden,
    kv_weight,
    kv_bias,
    memory_sections,
    group_sections,
    queries,
    new_keys,
    new_values,
    cache_keys,
    cache_values,
    cache_lengths,
    out_weight,
):
    mdev, feat = memory_hidden.shape
    heads = kv_weight.shape[2] // HD
    rows = queries.shape[0]
    qp = up(PER * rows + 1, 16)
    ar = up(heads * PER * rows, 16)
    ocols = out_weight.shape[1]
    orows = dp * rows // tp
    chunks = feat // 256 if feat % 256 == 0 else 1
    cuts = ocols // HD if ocols % HD == 0 else 1
    any_spec = pl.BlockSpec(memory_space=pl.ANY)
    smem = pl.BlockSpec(memory_space=pltpu.SMEM)
    dma = pltpu.SemaphoreType.DMA
    like = lambda a: pltpu.VMEM(a.shape, a.dtype)
    sections = memory_sections.reshape(1, -1)
    return pl.pallas_call(
        functools.partial(kernel, tp, dp),
        out_shape=jax.ShapeDtypeStruct((orows, ocols), BF16),
        in_specs=[smem, smem] + [any_spec] * 10,
        out_specs=pl.BlockSpec(memory_space=pltpu.VMEM),
        scratch_shapes=[
            pltpu.VMEM((tp, chunks, mdev, feat // chunks), BF16),
            like(kv_weight),
            like(kv_bias),
            like(sections),
            like(queries),
            like(new_keys),
            like(new_values),
            like(cache_keys),
            like(cache_values),
            like(out_weight),
            pltpu.VMEM((dp, heads, qp, HD), BF16),
            pltpu.VMEM((dp, ar, HD), BF16),
            pltpu.VMEM((dp, ar, HD), BF16),
            pltpu.VMEM((dp, 8, HD), F32),
            pltpu.VMEM((dp, 8, HD), F32),
            pltpu.VMEM((dp, ar, HD), BF16),
            pltpu.VMEM((tp, orows, ocols), F32),
            pltpu.VMEM((tp, orows * cuts, ocols // cuts), BF16),
            pltpu.VMEM((tp, orows * cuts, ocols // cuts), BF16),
            dma((9 + chunks,)),
            dma((tp, chunks)),
            dma((tp, chunks)),
        ]
        + [dma((dp,))] * 8
        + [dma((tp,))] * 2,
        compiler_params=pltpu.CompilerParams(
            collective_id=0, has_side_effects=True, vmem_limit_bytes=63 * 1024 * 1024
        ),
        name="decode_step",
    )(
        cache_lengths,
        group_sections,
        memory_hidden,
        kv_weight,
        kv_bias,
        sections,
        queries,
        new_keys,
        new_values,
        cache_keys,
        cache_values,
        out_weight,
    )


def solution(mesh):
    return jax.shard_map(
        functools.partial(body, mesh.shape["tp"], mesh.shape["dp"]),
        mesh=mesh,
        in_specs=(
            P(("parts", "dp"), "tp"),
            P(None, None, "tp"),
            P(None, "tp"),
            P("parts"),
            P(("parts", "dp")),
            P(("parts", "dp"), "tp"),
            P(("parts", "dp"), "tp"),
            P(("parts", "dp"), "tp"),
            P(("parts", "dp"), None, "tp"),
            P(("parts", "dp"), None, "tp"),
            P(("parts", "dp")),
            P("tp", "dp"),
        ),
        out_specs=P(("parts", "tp"), "dp"),
        check_vma=False,
    )
```

```python
import functools

import jax
import jax.numpy as jnp
from jax import lax
from jax.experimental import pallas as pl
from jax.experimental.pallas import tpu as pltpu
from jax.sharding import PartitionSpec as P

D = 5120
HQ = 40
KVH = 8
HD = 128
NEW = 2
LMAX = 512
PER = HQ // KVH
INV = 1.0 / HD**0.5
MASKED = -1e30
MESH = pl.DeviceIdType.MESH
F32 = jnp.float32
BF16 = jnp.bfloat16


def up(n, m):
    return -(-n // m) * m


def nt(a, b):
    return lax.dot_general(a, b, (((1,), (1,)), ((), ())), preferred_element_type=F32)


def tn(a, b):
    return lax.dot_general(a, b, (((0,), (0,)), ((), ())), preferred_element_type=F32)


def nn(a, b):
    return lax.dot_general(a, b, (((1,), (0,)), ((), ())), preferred_element_type=F32)


def kernel(
    tp,
    dp,
    lens,
    group,
    hidden_h,
    kvw_h,
    bias_h,
    sections_h,
    q_h,
    nk_h,
    nv_h,
    ck_h,
    cv_h,
    wo_h,
    out,
    hid,
    kvw,
    bias,
    sections,
    q_v,
    nk,
    nv,
    ck,
    cv,
    wo,
    qm,
    acc_s,
    acc_r,
    st_s,
    st_r,
    att,
    osum,
    osum_s,
    osum_r,
    load_sem,
    hid_ss,
    hid_rs,
    q_ss,
    q_rs,
    acc_ss,
    acc_rs,
    st_ss,
    st_rs,
    att_ss,
    att_rs,
    o_ss,
    o_rs,
):
    t = lax.axis_index("tp")
    d = lax.axis_index("dp")
    chunks, mdev, width = hid.shape[1:]
    feat = chunks * width
    relay = tp == 4
    rows, heads = q_v.shape[0], kvw.shape[2] // HD
    requests = ck.shape[0]
    qr = PER * rows
    qp = qm.shape[2]

    def at_tp(off):
        return {"tp": lax.rem(t + off, tp)}

    def at_dp(off):
        return {"dp": lax.rem(d + off + dp, dp)}

    barrier = pltpu.get_barrier_semaphore()
    for off in range(1, tp):
        pl.semaphore_signal(barrier, inc=1, device_id=at_tp(off), device_id_type=MESH)
    for off in range(1, dp):
        pl.semaphore_signal(barrier, inc=1, device_id=at_dp(off), device_id_type=MESH)

    pairs = (
        (q_h, q_v),
        (nk_h, nk),
        (nv_h, nv),
        (bias_h, bias),
        (sections_h, sections),
        (ck_h, ck),
        (cv_h, cv),
        (kvw_h, kvw),
        (wo_h, wo),
    ) + tuple(
        (hidden_h.at[:, c * width : (c + 1) * width], hid.at[0, c]) for c in range(chunks)
    )
    loads = [pltpu.make_async_copy(s, v, load_sem.at[i]) for i, (s, v) in enumerate(pairs)]
    l_q, l_nk, l_nv, l_bias, l_sec, l_ck, l_cv, l_kvw, l_wo = loads[:9]

    for copy in [l_q] + loads[9:] + [l_nk, l_nv, l_bias, l_sec, l_ck, l_cv, l_kvw]:
        copy.start()
    for copy in loads[9:]:
        copy.wait()
    pl.semaphore_wait(barrier, tp - 1 + dp - 1)

    def send(src, dst, ss, rs, to):
        copy = pltpu.make_async_remote_copy(
            src_ref=src, dst_ref=dst, send_sem=ss, recv_sem=rs, device_id=to, device_id_type=MESH
        )
        copy.start()
        return copy

    if relay:
        source = [t, t + 1 - 2 * lax.rem(t, 2), lax.rem(t + 2, tp), tp - 1 - t]
        direct = {2: source[2], 1: source[1]}
    else:
        source = [lax.rem(t - off + tp, tp) for off in range(tp)]
        direct = {off: lax.rem(t + off, tp) for off in range(1, tp)}
    hid_c = [[None] * chunks for _ in range(tp)]

    def send_hidden(slot, c, src, to):
        hid_c[slot][c] = send(
            src, hid.at[slot, c], hid_ss.at[slot, c], hid_rs.at[slot, c], {"tp": to}
        )

    def hand_on(c):
        if relay:
            hid_c[2][c].wait_recv()
            send_hidden(3, c, hid.at[2, c], source[1])

    for slot, to in direct.items():
        for c in range(chunks):
            send_hidden(slot, c, hid.at[0, c], to)

    l_wo.start()

    l_q.wait()
    q_wide = q_v[...].astype(F32)
    section_rows = jnp.full((qp - qr, HD), group[0], F32)
    for k in range(heads):
        parts = [q_wide[:, (k * PER + g) * HD : (k * PER + g + 1) * HD] for g in range(PER)]
        qm[0, k] = jnp.concatenate(parts + [section_rows], axis=0).astype(BF16)
    st_s[...] = jnp.zeros_like(st_s)

    q_c = [None] * dp
    for off in range(1, dp):
        q_c[off] = send(qm.at[0], qm.at[off], q_ss.at[off], q_rs.at[off], at_dp(off))

    for copy in (l_nk, l_nv, l_ck, l_cv, l_bias, l_sec):
        copy.wait()
    row = lax.broadcasted_iota(jnp.int32, (qr, 1), 0)
    token = lax.rem(row, rows)
    request = lax.div(token, NEW)
    slot = lax.broadcasted_iota(jnp.int32, (1, LMAX), 1)
    fresh = lax.broadcasted_iota(jnp.int32, (1, rows), 1)
    new_ok = (lax.div(fresh, NEW) == request) & (fresh <= token)
    own = []
    for k in range(heads):
        cols = slice(k * HD, (k + 1) * HD)
        qk = qm[0, k][:qr]
        scores = [jnp.where(new_ok, nt(qk, nk[:, cols]) * INV, MASKED)]
        for r in range(requests):
            ok = (request == r) & (slot < lens[r])
            scores.append(jnp.where(ok, nt(qk, ck[r, :, cols]) * INV, MASKED))
        top = functools.reduce(
            jnp.maximum, [jnp.max(s, axis=1, keepdims=True) for s in scores]
        )
        weights = [jnp.exp(s - top) for s in scores]
        total = functools.reduce(jnp.add, [jnp.sum(p, axis=1, keepdims=True) for p in weights])
        acc = nn(weights[0].astype(BF16), nv[:, cols])
        for r in range(requests):
            acc = acc + nn(weights[r + 1].astype(BF16), cv[r, :, cols])
        own.append((top, total, acc))
        if k < chunks:
            hand_on(k)

    l_kvw.wait()
    proj = [jnp.zeros((mdev, heads * HD), F32) for _ in range(2)]
    squares = jnp.zeros((mdev, 1), F32)
    handed = min(heads, chunks)
    for slot in range(tp):
        if relay and slot == 2:
            for c in range(handed, chunks):
                hand_on(c)
        for c in range(chunks):
            if slot and not (relay and slot == 2):
                hid_c[slot][c].wait_recv()
            piece = hid[slot, c]
            wide = piece.astype(F32)
            squares = squares + jnp.sum(wide * wide, axis=1, keepdims=True)
            first = pl.multiple_of(source[slot] * feat + c * width, width)
            for s in range(2):
                proj[s] = proj[s] + nn(piece, kvw[s, pl.ds(first, width), :])
    scale = lax.rsqrt(squares / D + 1e-06)
    mem_k, mem_v = [
        (proj[s] * scale + bias[s : s + 1, :].astype(F32)).astype(BF16) for s in range(2)
    ]

    mrows = sections.shape[1]
    lane = lax.broadcasted_iota(jnp.int32, (mdev, mrows), 1)
    place = lax.broadcasted_iota(jnp.int32, (mdev, mrows), 0) + d * mdev
    mine = jnp.where(lane == place, sections[...].astype(F32), 0.0)
    section = jnp.sum(mine, axis=1, keepdims=True)
    ar = att.shape[1]

    def pack(blocks):
        if ar > heads * qr:
            blocks = blocks + [jnp.zeros((ar - heads * qr, HD), F32)]
        return jnp.concatenate(blocks, axis=0).astype(BF16)

    acc_c = [None] * dp
    st_c = [None] * dp
    for off in list(range(1, dp)) + [0]:
        if off:
            q_c[off].wait_recv()
        sums = []
        for k in range(heads):
            cols = slice(k * HD, (k + 1) * HD)
            qk = qm[off, k]
            ok = section == qk[qr : qr + 1, 0:1].astype(F32)
            s = jnp.where(ok, nt(mem_k[:, cols], qk) * INV, MASKED)
            top = jnp.max(s, axis=0, keepdims=True)
            p = jnp.where(ok, jnp.exp(s - top), 0.0)
            sums.append(tn(p.astype(BF16), mem_v[:, cols])[:qr])
            st_s[off, 2 * k : 2 * k + 1, 0:qp] = top
            st_s[off, 2 * k + 1 : 2 * k + 2, 0:qp] = jnp.sum(p, axis=0, keepdims=True)
        acc_s[off] = pack(sums)
        if off:
            st_c[off] = send(st_s.at[off], st_r.at[off], st_ss.at[off], st_rs.at[off], at_dp(-off))
            acc_c[off] = send(
                acc_s.at[off], acc_r.at[off], acc_ss.at[off], acc_rs.at[off], at_dp(-off)
            )

    def merge(state, offs):
        stats = [jnp.transpose((st_r if off else st_s)[off]) for off in offs]
        terms = [(acc_r if off else acc_s)[off].astype(F32) for off in offs]
        merged = []
        for k in range(heads):
            top_c, total_c, acc = state[k]
            tops = [st[:qr, 2 * k : 2 * k + 1] for st in stats]
            top = functools.reduce(jnp.maximum, tops, top_c)
            factor = jnp.exp(top_c - top)
            total = total_c * factor
            acc = acc * factor
            for i in range(len(offs)):
                factor = jnp.exp(tops[i] - top)
                total = total + stats[i][:qr, 2 * k + 1 : 2 * k + 2] * factor
                acc = acc + terms[i][k * qr : (k + 1) * qr] * factor
            merged.append((top, total, acc))
        return merged

    own = merge(own, [0])
    for off in range(1, dp):
        st_c[off].wait_recv()
        acc_c[off].wait_recv()
    own = merge(own, list(range(1, dp)))
    att[0] = pack([acc / total for _, total, acc in own])
    att_c = [None] * dp
    for off in range(1, dp):
        att_c[off] = send(att.at[0], att.at[off], att_ss.at[off], att_rs.at[off], at_dp(off))

    l_wo.wait()
    for off in range(1, dp):
        att_c[off].wait_recv()
    groups = []
    for g in range(dp):
        a = att[lax.rem(d - g + dp, dp)].astype(F32)
        groups.append(
            jnp.concatenate([a[h * rows : (h + 1) * rows] for h in range(heads * PER)], axis=1)
        )
    lhs = jnp.concatenate(groups, axis=0).astype(BF16)
    orows, ocols = osum.shape[1:]
    cuts = osum_s.shape[1] // orows
    span = ocols // cuts
    result = nn(lhs, wo[...])
    for i in range(tp):
        mine = result[i * orows : (i + 1) * orows]
        osum[i] = mine
        osum_s[i] = jnp.concatenate(
            [mine[:, c * span : (c + 1) * span] for c in range(cuts)], axis=0
        ).astype(BF16)
    o_c = [None] * tp
    for off in range(1, tp):
        to = lax.rem(t + off, tp)
        o_c[off] = send(osum_s.at[to], osum_r.at[off], o_ss.at[off], o_rs.at[off], at_tp(off))
    own_sum = osum[t]
    summed = [own_sum[:, c * span : (c + 1) * span] for c in range(cuts)]
    for off in range(1, tp):
        o_c[off].wait_recv()
        came = osum_r[off].astype(F32)
        summed = [v + came[c * orows : (c + 1) * orows] for c, v in enumerate(summed)]
    out[...] = jnp.concatenate(summed, axis=1).astype(BF16)

    for copies in hid_c + [q_c, st_c, acc_c, att_c, o_c]:
        for copy in copies:
            if copy is not None:
                copy.wait_send()


def body(
    tp,
    dp,
    memory_hidden,
    kv_weight,
    kv_bias,
    memory_sections,
    group_sections,
    queries,
    new_keys,
    new_values,
    cache_keys,
    cache_values,
    cache_lengths,
    out_weight,
):
    mdev, feat = memory_hidden.shape
    heads = kv_weight.shape[2] // HD
    rows = queries.shape[0]
    qp = up(PER * rows + 1, 16)
    ar = up(heads * PER * rows, 16)
    ocols = out_weight.shape[1]
    orows = dp * rows // tp
    chunks = feat // 640 if feat % 640 == 0 else 1
    cuts = ocols // HD if ocols % HD == 0 else 1
    any_spec = pl.BlockSpec(memory_space=pl.ANY)
    smem = pl.BlockSpec(memory_space=pltpu.SMEM)
    dma = pltpu.SemaphoreType.DMA
    like = lambda a: pltpu.VMEM(a.shape, a.dtype)
    sections = memory_sections.reshape(1, -1)
    return pl.pallas_call(
        functools.partial(kernel, tp, dp),
        out_shape=jax.ShapeDtypeStruct((orows, ocols), BF16),
        in_specs=[smem, smem] + [any_spec] * 10,
        out_specs=pl.BlockSpec(memory_space=pltpu.VMEM),
        scratch_shapes=[
            pltpu.VMEM((tp, chunks, mdev, feat // chunks), BF16),
            like(kv_weight),
            like(kv_bias),
            like(sections),
            like(queries),
            like(new_keys),
            like(new_values),
            like(cache_keys),
            like(cache_values),
            like(out_weight),
            pltpu.VMEM((dp, heads, qp, HD), BF16),
            pltpu.VMEM((dp, ar, HD), BF16),
            pltpu.VMEM((dp, ar, HD), BF16),
            pltpu.VMEM((dp, 8, HD), F32),
            pltpu.VMEM((dp, 8, HD), F32),
            pltpu.VMEM((dp, ar, HD), BF16),
            pltpu.VMEM((tp, orows, ocols), F32),
            pltpu.VMEM((tp, orows * cuts, ocols // cuts), BF16),
            pltpu.VMEM((tp, orows * cuts, ocols // cuts), BF16),
            dma((9 + chunks,)),
            dma((tp, chunks)),
            dma((tp, chunks)),
        ]
        + [dma((dp,))] * 8
        + [dma((tp,))] * 2,
        compiler_params=pltpu.CompilerParams(
            collective_id=0, has_side_effects=True, vmem_limit_bytes=63 * 1024 * 1024
        ),
        name="decode_step",
    )(
        cache_lengths,
        group_sections,
        memory_hidden,
        kv_weight,
        kv_bias,
        sections,
        queries,
        new_keys,
        new_values,
        cache_keys,
        cache_values,
        out_weight,
    )


def solution(mesh):
    return jax.shard_map(
        functools.partial(body, mesh.shape["tp"], mesh.shape["dp"]),
        mesh=mesh,
        in_specs=(
            P(("parts", "dp"), "tp"),
            P(None, None, "tp"),
            P(None, "tp"),
            P("parts"),
            P(("parts", "dp")),
            P(("parts", "dp"), "tp"),
            P(("parts", "dp"), "tp"),
            P(("parts", "dp"), "tp"),
            P(("parts", "dp"), None, "tp"),
            P(("parts", "dp"), None, "tp"),
            P(("parts", "dp")),
            P("tp", "dp"),
        ),
        out_specs=P(("parts", "tp"), "dp"),
        check_vma=False,
    )
```
